256 devices in a mesh: tx: 8 (over z), ty: 16 (over x, y), scan: 2 (over core).
Axes of the slice: x: 4, y: 4, z: 8, core: 2. Of those that a mesh axis runs over, the one named last changes fastest.
Arguments:
- object_slices: float32 [2, 2, 4096, 8192], P(None, None, 'tx', 'ty'), may hold values from -3 to 3
- probe_modes: float32 [2, 2, 256, 256], replicated, may hold values from -5 to 5
- offsets: int32 [256, 2], P(('tx', 'ty', 'scan')), may hold values from 0 to 511, as said below
- measured: float32 [256, 256, 256], P(('tx', 'ty', 'scan')), may hold values from 0.25 to 8
Outputs:
- object_grad: float32 [2, 2, 4096, 8192], P(None, None, 'tx', 'ty')
- probe_grad: float32 [2, 2, 256, 256], replicated
The draws below stay inside these ranges and needn't reach their ends.
Inputs may be any that keep to these rules, and one draw needn't show every extreme that they name: `offsets`: the position is held by the device of its tile; every patch lies inside the object, so in the last tile row the row offset is at most 256 and in the last tile column the column offset is at most 256.
All inputs are finite; a program needn't handle non-finite values.
Results may differ from the reference program's by a relative error of at most 0.0003.
Values sent between devices are 32-bit elements; how exact they have to be, the bound alone decides.
No kernel may reach another device: no remote copies, remote signals or barrier semaphores. Data moves between devices by JAX's collectives and lax.ppermute only.
A program may use at most 128 MiB of HBM per device.

```python
import math
import jax
import jax.numpy as jnp
from jax import lax

P_SIZE = 256
M = 2
NSLICE = 2
CR = 512
CC = 512
POS_DEV = 1
POSITIONS = 256
NROWS = 4096
NCOLS = 8192
N_TX = 8
N_TY = 16
N_SCAN = 2


def draw_offsets(key, part):
    key = jax.random.fold_in(key, 7)
    positions = jnp.arange(POSITIONS, dtype=jnp.int32)
    tile_row = positions // (N_TY * N_SCAN * POS_DEV)
    tile_col = positions // (N_SCAN * POS_DEV) % N_TY
    row_limit = jnp.where(tile_row == N_TX - 1, CR - P_SIZE + 1, CR)
    col_limit = jnp.where(tile_col == N_TY - 1, CC - P_SIZE + 1, CC)
    row_key, col_key = jax.random.split(key)
    row_offset = jax.random.randint(row_key, (POSITIONS,), 0, row_limit)
    col_offset = jax.random.randint(col_key, (POSITIONS,), 0, col_limit)
    first = positions == 0
    row_offset = jnp.where(first, CR - 1, row_offset)
    col_offset = jnp.where(first, CC - 1, col_offset)
    return jnp.stack([row_offset, col_offset], axis=1).astype(jnp.int32)


def block_levels(own_key, shape, cuts, smallest, largest):
    level = 1.0
    for axis_at, shards_of in cuts:
        draws = jax.random.uniform(jax.random.fold_in(jax.random.fold_in(own_key, 6), axis_at), (shards_of,), jnp.float32, smallest / len(cuts), largest / len(cuts))
        level = level * jnp.repeat(jnp.exp(draws), shape[axis_at] // shards_of).reshape((-1,) + (1,) * (len(shape) - 1 - axis_at))
    return level


def normal_values(rng, shape, scale, most, cuts=(), kind=jnp.bfloat16):
    values = jax.random.normal(rng, shape, jnp.float32) * scale
    if len(cuts) > 0:
        values = block_levels(rng, shape, cuts, -0.22, 0.18) * values
    return jnp.clip(values, min=-most, max=most).astype(kind)


def setup_inputs(seed: int = 0) -> dict:
    seeds = jax.random.split(jax.random.key(seed), 5)
    object_slices = normal_values(seeds[0], (NSLICE, 2, NROWS, NCOLS), 0.7, 3.0, ((2, 8), (3, 16)), jnp.float32)
    probe_modes = normal_values(seeds[1], (M, 2, P_SIZE, P_SIZE), 1.0, 5.0, (), jnp.float32)
    offsets = draw_offsets(jax.random.fold_in(seeds[4], 71), 0)
    measured = jnp.clip(jnp.exp(math.log(8.0) - 3.465736 * jax.random.uniform(seeds[3], (POSITIONS, P_SIZE, P_SIZE), jnp.float32) ** block_levels(seeds[3], (POSITIONS, P_SIZE, P_SIZE), ((0, 256),), -0.2, 0.2)), 0.25, 8.0)
    return dict(object_slices=object_slices, probe_modes=probe_modes, offsets=offsets, measured=measured)


fresnel_number = 6.0

def chirp_phase(extent):
    freqs = (jnp.arange(extent, dtype=jnp.int32) + extent // 2) % extent - extent // 2
    squares = (freqs * freqs).astype(jnp.float32)
    return jnp.pi * fresnel_number * (squares[:, None] + squares[None, :]) / float(extent * extent)

def position_error(cells, modes, target):
    layers = cells[:, 0] + 1j * cells[:, 1]
    waves = (modes[:, 0] + 1j * modes[:, 1]) * layers[0]
    kernel = jnp.exp(-1j * chirp_phase(P_SIZE))
    for layer_index in range(1, NSLICE):
        spectrum = jnp.fft.fft2(waves, norm='ortho')
        waves = jnp.fft.ifft2(kernel * spectrum, norm='ortho') * layers[layer_index]
    far_field = jnp.fft.fft2(waves, norm='ortho')
    intensity = lax.optimization_barrier(jnp.sum(jnp.real(far_field) ** 2 + jnp.imag(far_field) ** 2, axis=0))
    return 0.5 * jnp.sum((intensity - target) ** 2)

def reference(object_slices, probe_modes, offsets, measured):
    per_group = N_TY * N_SCAN * POS_DEV

    def visit(carry, inputs):
        grad_field, grad_modes = carry
        position, shift_pair, target = inputs
        tile_row = position // per_group
        tile_col = position // (N_SCAN * POS_DEV) % N_TY
        row_start = (tile_row * CR + shift_pair[0]).astype(jnp.int32)
        col_start = (tile_col * CC + shift_pair[1]).astype(jnp.int32)
        zero = jnp.int32(0)
        starts = (zero, zero, row_start, col_start)
        cells = lax.dynamic_slice(object_slices, starts, (NSLICE, 2, P_SIZE, P_SIZE))
        value, pullback = jax.vjp(lambda cells_in, modes_in: position_error(cells_in, modes_in, target), cells, probe_modes)
        grad_cells, grad_probe = pullback(jnp.ones_like(value))
        current = lax.dynamic_slice(grad_field, starts, (NSLICE, 2, P_SIZE, P_SIZE))
        grad_field = lax.dynamic_update_slice(grad_field, current + grad_cells, starts)
        return ((grad_field, grad_modes + grad_probe), None)
    positions = jnp.arange(POSITIONS, dtype=jnp.int32)
    start_state = (jnp.zeros_like(object_slices), jnp.zeros_like(probe_modes))
    (grad_field, grad_modes), _ = lax.scan(visit, start_state, (positions, offsets, measured))
    return (grad_field, grad_modes / POSITIONS)
```

```python
import functools
import math

import jax
import jax.numpy as jnp
import ml_dtypes
import numpy as np
from jax import lax
from jax.experimental import pallas as pl
from jax.experimental.pallas import tpu as pltpu
from jax.sharding import PartitionSpec as P

fresnel_number = 6.0
W = 256
B16 = jnp.bfloat16
F32 = jnp.float32


def real_form(matrix):
    return np.block([[matrix.real, -matrix.imag], [matrix.imag, matrix.real]])


def tables():
    half = W // 2
    n = np.arange(half)
    norm = 1.0 / math.sqrt(W)
    even = np.exp(-2j * np.pi * np.outer(2 * n, n) / W) * norm
    odd = np.exp(-2j * np.pi * np.outer(2 * n + 1, n) / W) * norm
    k = np.arange(W)
    q = (k + half) % W - half
    h = np.exp(-1j * np.pi * fresnel_number * q.astype(np.float64) ** 2 / float(W * W))
    taps = np.fft.ifft(h)
    diff = (n[:, None] - n[None, :]) % W
    near, far = taps[diff], taps[(diff + half) % W]
    mats = [even, odd, 0.5 * (near + far), 0.5 * (near - far)]
    forms = []
    for m in mats:
        r = real_form(m)
        forms += [r, r.T]
    full = np.stack(forms)
    hi = full.astype(ml_dtypes.bfloat16)
    lo = (full - hi.astype(np.float64)).astype(ml_dtypes.bfloat16)
    return np.stack([hi, lo], axis=1)


E_L, E_T, O_L, O_T, U_L, U_T, V_L, V_T = range(8)


def deinterleave():
    order = np.concatenate([np.arange(0, W, 2), np.arange(1, W, 2)])
    p = np.zeros((W, W), np.float32)
    p[np.arange(W), order] = 1.0
    return np.stack([p, p.T]).astype(ml_dtypes.bfloat16)


def dot(a, b):
    return jnp.dot(a, b, preferred_element_type=F32)


def split(x):
    hi = x.astype(B16)
    return hi, (x - hi.astype(F32)).astype(B16)


def times(tab, which, x, axis):
    hi, lo = split(x)
    t_hi, t_lo = tab[which, 0], tab[which, 1]
    if axis == 0:
        return dot(t_hi, hi) + (dot(t_hi, lo) + dot(t_lo, hi))
    return dot(hi, t_hi) + (dot(lo, t_hi) + dot(hi, t_lo))


def halves(x, axis):
    h = W // 2
    return (x[:h], x[h:]) if axis == 0 else (x[:, :h], x[:, h:])


def butterfly(re, im, axis):
    r0, r1 = halves(re, axis)
    i0, i1 = halves(im, axis)
    u = jnp.concatenate([r0 + r1, i0 + i1], axis)
    v = jnp.concatenate([r0 - r1, i0 - i1], axis)
    return u, v


def join(a, b, axis):
    ar, ai = halves(a, axis)
    br, bi = halves(b, axis)
    return jnp.concatenate([ar, br], axis), jnp.concatenate([ai, bi], axis)


def one_axis(tab, kind, re, im, axis):
    left = axis == 0
    if kind == "inv":
        r0, r1 = halves(re, axis)
        i0, i1 = halves(im, axis)
        u, v = jnp.concatenate([r0, i0], axis), jnp.concatenate([r1, i1], axis)
    else:
        u, v = butterfly(re, im, axis)
    pick = {
        "fwd": (E_L, O_L) if left else (E_T, O_T),
        "inv": (E_T, O_T) if left else (E_L, O_L),
        "prop": (U_L, V_L) if left else (U_T, V_T),
        "back": (U_T, V_T) if left else (U_L, V_L),
    }[kind]
    a = times(tab, pick[0], u, axis)
    b = times(tab, pick[1], v, axis)
    if kind != "fwd":
        a, b = a + b, a - b
    return join(a, b, axis)


def both_axes(tab, kind, re, im):
    re, im = one_axis(tab, kind, re, im, 0)
    return one_axis(tab, kind, re, im, 1)


def cmul(ar, ai, br, bi):
    return ar * br - ai * bi, ar * bi + ai * br


def cmul_conj(ar, ai, br, bi):
    return ar * br + ai * bi, ar * bi - ai * br


def iotas():
    return (
        lax.broadcasted_iota(jnp.int32, (W, W), 0),
        lax.broadcasted_iota(jnp.int32, (W, W), 1),
    )


def block(q):
    return pl.ds(pl.multiple_of(q * W, W), W)


def prep_kernel(off, obj, probe, meas, perm, own_out, probe_out, meas_out):
    qr, tr = off[0] // W, off[0] % W
    qc, tc = off[1] // W, off[1] % W
    rho, gam = iotas()
    low_r, low_c = rho < tr, gam < tc
    for layer in range(2):
        for p in range(2):
            a = jnp.where(low_c, obj[layer, p, block(qr), W:], obj[layer, p, block(qr), block(qc)])
            b = jnp.where(low_c, obj[layer, p, W:, W:], obj[layer, p, W:, block(qc)])
            own_out[layer, p] = jnp.where(low_r, b, a)
    for m in range(2):
        for p in range(2):
            x = pltpu.roll(probe[m, p], tr, 0)
            probe_out[m, p] = pltpu.roll(x, tc, 1)

    def exact(x):
        hi, rest = x.astype(B16), None
        rest = x - hi.astype(F32)
        mid = rest.astype(B16)
        low = (rest - mid.astype(F32)).astype(B16)
        return hi, mid, low

    hi, mid, low = exact(meas[...])
    x = dot(perm[0], hi) + dot(perm[0], mid) + dot(perm[0], low)
    hi, mid, low = exact(x)
    meas_out[...] = dot(hi, perm[1]) + dot(mid, perm[1]) + dot(low, perm[1])


def whole_patch(off, own, below, right, diag):
    qr, tr = off[0] // W, off[0] % W
    qc, tc = off[1] // W, off[1] % W
    rho, gam = iotas()
    low_r, low_c = rho < tr, gam < tc
    halo_r = rho < tr * qr
    halo_c = gam < tc * qc
    below_v = jnp.where(low_c, below[:, W:], below[:, block(qc)])
    right_v = jnp.where(low_r, right[W:, :], right[block(qr), :])
    out = jnp.where(halo_r, below_v, own)
    return jnp.where(halo_c, jnp.where(halo_r, diag[...], right_v), out)


def patch_planes(scal, own, halo_mine, halo_other, out):
    s = scal[2]
    out[s] = whole_patch(scal, own[s], *halo_mine)
    out[1 - s] = whole_patch(scal, own[1 - s], *halo_other)


def first_kernel(scal, own, b0, r0, d0, b1, r1, d1, probe, tab, obj_out, back_out):
    patch_planes(scal, own, (b0, r0, d0), (b1, r1, d1), obj_out)
    o_r, o_i = obj_out[0], obj_out[1]
    for m in range(2):
        re, im = cmul(probe[m, 0], probe[m, 1], o_r, o_i)
        re, im = both_axes(tab, "prop", re, im)
        back_out[m, 0] = re
        back_out[m, 1] = im


def middle_kernel(scal, own, b0, r0, d0, b1, r1, d1, back, meas, tab, grad_out, wave_out, obj, far):
    patch_planes(scal, own, (b0, r0, d0), (b1, r1, d1), obj)
    for m in range(2):
        re, im = cmul(back[m, 0], back[m, 1], obj[0], obj[1])
        re, im = both_axes(tab, "fwd", re, im)
        far[m, 0] = re
        far[m, 1] = im
    inten = far[0, 0] ** 2 + far[0, 1] ** 2 + far[1, 0] ** 2 + far[1, 1] ** 2
    resid = 2.0 * (inten - meas[...])
    g_r = g_i = None
    for m in range(2):
        re, im = both_axes(tab, "inv", resid * far[m, 0], resid * far[m, 1])
        a, b = cmul_conj(back[m, 0], back[m, 1], re, im)
        g_r, g_i = (a, b) if g_r is None else (g_r + a, g_i + b)
        wave_out[m, 0], wave_out[m, 1] = cmul_conj(obj[0], obj[1], re, im)
    grad_out[0] = g_r
    grad_out[1] = g_i


def last_kernel(scal, wave, obj, probe, tab, grad_out, probe_out):
    tr, tc = scal[0] % W, scal[1] % W
    g_r = g_i = None
    for m in range(2):
        re, im = both_axes(tab, "back", wave[m, 0], wave[m, 1])
        a, b = cmul_conj(probe[m, 0], probe[m, 1], re, im)
        g_r, g_i = (a, b) if g_r is None else (g_r + a, g_i + b)
        for p, x in enumerate(cmul_conj(obj[0], obj[1], re, im)):
            x = pltpu.roll(x * (1.0 / 256.0), (W - tr) % W, 0)
            probe_out[m, p] = pltpu.roll(x, (W - tc) % W, 1)
    grad_out[0] = g_r
    grad_out[1] = g_i


def spread_kernel(scal, mine, other, own_out, below_out, right_out, diag_out):
    rho, gam = iotas()

    def band(index, q, t, i):
        return ((index >= t) & (q == i)) | ((index < t) & (q + 1 == i))

    where = []
    for k in range(2):
        r, c = scal[2 * k], scal[2 * k + 1]
        rows = [band(rho, r // W, r % W, i) for i in range(3)]
        cols = [band(gam, c // W, c % W, j) for j in range(3)]
        where.append((rows, cols))
    a, b = mine[...], other[...]
    for i in range(3):
        for j in range(3):
            v = jnp.where(where[0][0][i] & where[0][1][j], a, 0.0) + jnp.where(
                where[1][0][i] & where[1][1][j], b, 0.0
            )
            if i < 2 and j < 2:
                own_out[i * W : (i + 1) * W, j * W : (j + 1) * W] = v
            elif i < 2:
                right_out[i * W : (i + 1) * W, :] = v
            elif j < 2:
                below_out[:, j * W : (j + 1) * W] = v
            else:
                diag_out[...] = v


def finish_kernel(scal, own0, b0, r0, d0, own1, b1, r1, d1, out):
    s = scal[0]
    for plane, own, b, r, d in ((s, own0, b0, r0, d0), (1 - s, own1, b1, r1, d1)):
        out[plane, W:, W:] = own[W:, W:]
        out[plane, :W, :W] = own[:W, :W] + (b[:, :W] + r[:W, :] + d[...])
        out[plane, :W, W:] = own[:W, W:] + b[:, W:]
        out[plane, W:, :W] = own[W:, :W] + r[W:, :]


def call(kernel, outs, args, flops=0, scratch=()):
    spec = pl.BlockSpec(memory_space=pltpu.VMEM)
    moved = 4 * sum(math.prod(o) for o in outs) + sum(a.size * a.dtype.itemsize for a in args)
    return pl.pallas_call(
        kernel,
        out_shape=[jax.ShapeDtypeStruct(o, F32) for o in outs],
        in_specs=[pl.BlockSpec(memory_space=pltpu.SMEM)] + [spec] * (len(args) - 1),
        out_specs=[spec] * len(outs),
        scratch_shapes=[pltpu.VMEM(s, F32) for s in scratch],
        compiler_params=pltpu.CompilerParams(vmem_limit_bytes=40 * 2**20),
        cost_estimate=pl.CostEstimate(flops=flops, bytes_accessed=moved, transcendentals=0),
    )(*args)


def swap(x):
    return lax.ppermute(x, "scan", [(0, 1), (1, 0)])


def shift(x, rows, cols):
    n_a, n_b = lax.axis_size("tx"), lax.axis_size("ty")
    route = [
        (a * n_b + b, (a + rows) * n_b + b + cols)
        for a in range(n_a)
        for b in range(n_b)
        if 0 <= a + rows < n_a and 0 <= b + cols < n_b
    ]
    return lax.ppermute(x, ("tx", "ty"), route)


def at(v, i):
    return lax.dynamic_index_in_dim(v, i, 0, keepdims=False)


def along(kind):
    def move(x, d):
        if kind == "x":
            route = [(i, ((i // 4 + d) % 4) * 4 + i % 4) for i in range(16)]
        else:
            route = [(i, (i // 4) * 4 + (i + d) % 4) for i in range(16)]
        return lax.ppermute(x, "ty", route)

    return move


def scatter_sum(v, index, n, move):
    got = [move(at(v, (index + d) % n), d) for d in range(1, n)]
    total = at(v, index)
    for g in got:
        total = total + g
    return total


def gather(v, index, n, move):
    got = [v] + [move(v, d) for d in range(1, n)]
    out = jnp.zeros((n,) + v.shape, v.dtype)
    for d, g in enumerate(got):
        out = lax.dynamic_update_index_in_dim(out, g, (index - d) % n, 0)
    return out


def sum_everywhere(grads, s):
    col = lax.axis_index("ty")
    x, y = col // 4, col % 4
    v = at(grads, s) + swap(at(grads, 1 - s))
    v = scatter_sum(v.reshape(4, 128, W), x, 4, along("x"))
    v = scatter_sum(v.reshape(4, 32, W), y, 4, along("y"))
    for bit in (1, 2, 4):
        v = v + lax.ppermute(v, "tx", [(i, i ^ bit) for i in range(8)])
    v = gather(v, y, 4, along("y")).reshape(128, W)
    v = gather(v, x, 4, along("x")).reshape(2, W, W)
    other = swap(v)
    return jnp.where(s == 0, jnp.stack([v, other]), jnp.stack([other, v]))


def body(object_slices, probe_modes, offsets, measured):
    s = lax.axis_index("scan").astype(jnp.int32)
    tab = jnp.asarray(tables())
    perm = jnp.asarray(deinterleave())

    halos = []
    for layer in range(2):
        plane = at(object_slices[layer], s)
        mine = (
            shift(plane[:W, :], -1, 0),
            shift(plane[:, :W], 0, -1),
            shift(plane[:W, :W], -1, -1),
        )
        halos.append(mine + tuple(swap(h) for h in mine))

    off = offsets.reshape(2)
    off_other = swap(off)
    scal = jnp.concatenate([off, s[None]])
    pair = jnp.concatenate([off, off_other])

    own, probe, meas = call(
        prep_kernel,
        [(2, 2, W, W), (2, 2, W, W), (W, W)],
        (off, object_slices, probe_modes, measured[0], perm),
        flops=12 * W**3,
    )
    obj0, back = call(
        first_kernel,
        [(2, W, W), (2, 2, W, W)],
        (scal, own[0], *halos[0], probe, tab),
        flops=48 * W**3,
    )
    grad1, wave = call(
        middle_kernel,
        [(2, W, W), (2, 2, W, W)],
        (scal, own[1], *halos[1], back, meas, tab),
        flops=96 * W**3,
        scratch=[(2, W, W), (2, 2, W, W)],
    )
    grad0, grad_probe = call(
        last_kernel,
        [(2, W, W), (2, 2, W, W)],
        (scal, wave, obj0, probe, tab),
        flops=48 * W**3,
    )

    def out(grad):
        own_sum, below, right, diag = call(
            spread_kernel,
            [(2 * W, 2 * W), (W, 2 * W), (2 * W, W), (W, W)],
            (pair, at(grad, s), swap(at(grad, 1 - s))),
        )
        mine = (shift(below, 1, 0), shift(right, 0, 1), shift(diag, 1, 1))
        other = tuple(swap(h) for h in mine)
        return call(
            finish_kernel,
            [(2, 2 * W, 2 * W)],
            (s[None], own_sum, *mine, swap(own_sum), *other),
        )[0]

    tile1 = out(grad1)
    tile0 = out(grad0)
    return jnp.stack([tile0, tile1]), sum_everywhere(grad_probe, s)


def solution(mesh):
    placed = (
        P(None, None, "tx", "ty"),
        P(),
        P(("tx", "ty", "scan"), None),
        P(("tx", "ty", "scan"), None, None),
    )
    return jax.shard_map(
        body,
        mesh=mesh,
        in_specs=placed,
        out_specs=(P(None, None, "tx", "ty"), P()),
        check_vma=False,
    )
```

```python
import functools
import math

import jax
import jax.numpy as jnp
import ml_dtypes
import numpy as np
from jax import lax
from jax.experimental import pallas as pl
from jax.experimental.pallas import tpu as pltpu
from jax.sharding import PartitionSpec as P

fresnel_number = 6.0
W = 256
B16 = jnp.bfloat16
F32 = jnp.float32


def real_form(matrix):
    return np.block([[matrix.real, -matrix.imag], [matrix.imag, matrix.real]])


def tables():
    half = W // 2
    n = np.arange(half)
    norm = 1.0 / math.sqrt(W)
    even = np.exp(-2j * np.pi * np.outer(2 * n, n) / W) * norm
    odd = np.exp(-2j * np.pi * np.outer(2 * n + 1, n) / W) * norm
    k = np.arange(W)
    q = (k + half) % W - half
    h = np.exp(-1j * np.pi * fresnel_number * q.astype(np.float64) ** 2 / float(W * W))
    taps = np.fft.ifft(h)
    diff = (n[:, None] - n[None, :]) % W
    near, far = taps[diff], taps[(diff + half) % W]
    mats = [even, odd, 0.5 * (near + far), 0.5 * (near - far)]
    forms = []
    for m in mats:
        r = real_form(m)
        forms += [r, r.T]
    full = np.stack(forms)
    hi = full.astype(ml_dtypes.bfloat16)
    lo = (full - hi.astype(np.float64)).astype(ml_dtypes.bfloat16)
    return np.stack([hi, lo], axis=1)


E_L, E_T, O_L, O_T, U_L, U_T, V_L, V_T = range(8)


def deinterleave():
    order = np.concatenate([np.arange(0, W, 2), np.arange(1, W, 2)])
    p = np.zeros((W, W), np.float32)
    p[np.arange(W), order] = 1.0
    return np.stack([p, p.T]).astype(ml_dtypes.bfloat16)


def dot(a, b):
    return jnp.dot(a, b, preferred_element_type=F32)


def split(x):
    hi = x.astype(B16)
    return hi, (x - hi.astype(F32)).astype(B16)


def times(tab, which, x, axis):
    hi, lo = split(x)
    t_hi, t_lo = tab[which, 0], tab[which, 1]
    if axis == 0:
        return dot(t_hi, hi) + (dot(t_hi, lo) + dot(t_lo, hi))
    return dot(hi, t_hi) + (dot(lo, t_hi) + dot(hi, t_lo))


def halves(x, axis):
    h = W // 2
    return (x[:h], x[h:]) if axis == 0 else (x[:, :h], x[:, h:])


def butterfly(re, im, axis):
    r0, r1 = halves(re, axis)
    i0, i1 = halves(im, axis)
    u = jnp.concatenate([r0 + r1, i0 + i1], axis)
    v = jnp.concatenate([r0 - r1, i0 - i1], axis)
    return u, v


def join(a, b, axis):
    ar, ai = halves(a, axis)
    br, bi = halves(b, axis)
    return jnp.concatenate([ar, br], axis), jnp.concatenate([ai, bi], axis)


def one_axis(tab, kind, re, im, axis):
    left = axis == 0
    if kind == "inv":
        r0, r1 = halves(re, axis)
        i0, i1 = halves(im, axis)
        u, v = jnp.concatenate([r0, i0], axis), jnp.concatenate([r1, i1], axis)
    else:
        u, v = butterfly(re, im, axis)
    pick = {
        "fwd": (E_L, O_L) if left else (E_T, O_T),
        "inv": (E_T, O_T) if left else (E_L, O_L),
        "prop": (U_L, V_L) if left else (U_T, V_T),
        "back": (U_T, V_T) if left else (U_L, V_L),
    }[kind]
    a = times(tab, pick[0], u, axis)
    b = times(tab, pick[1], v, axis)
    if kind != "fwd":
        a, b = a + b, a - b
    return join(a, b, axis)


def both_axes(tab, kind, re, im):
    re, im = one_axis(tab, kind, re, im, 0)
    return one_axis(tab, kind, re, im, 1)


def cmul(ar, ai, br, bi):
    return ar * br - ai * bi, ar * bi + ai * br


def cmul_conj(ar, ai, br, bi):
    return ar * br + ai * bi, ar * bi - ai * br


def iotas():
    return (
        lax.broadcasted_iota(jnp.int32, (W, W), 0),
        lax.broadcasted_iota(jnp.int32, (W, W), 1),
    )


def block(q):
    return pl.ds(pl.multiple_of(q * W, W), W)


def prep_kernel(off, obj, probe, meas, perm, own_out, probe_out, meas_out):
    qr, tr = off[0] // W, off[0] % W
    qc, tc = off[1] // W, off[1] % W
    rho, gam = iotas()
    low_r, low_c = rho < tr, gam < tc
    for layer in range(2):
        for p in range(2):
            a = jnp.where(low_c, obj[layer, p, block(qr), W:], obj[layer, p, block(qr), block(qc)])
            b = jnp.where(low_c, obj[layer, p, W:, W:], obj[layer, p, W:, block(qc)])
            own_out[layer, p] = jnp.where(low_r, b, a)
    for m in range(2):
        for p in range(2):
            x = pltpu.roll(probe[m, p], tr, 0)
            probe_out[m, p] = pltpu.roll(x, tc, 1)

    def exact(x):
        hi = x.astype(B16)
        rest = x - hi.astype(F32)
        mid = rest.astype(B16)
        return hi, mid, (rest - mid.astype(F32)).astype(B16)

    hi, mid, low = exact(meas[...])
    x = dot(perm[0], hi) + dot(perm[0], mid) + dot(perm[0], low)
    hi, mid, low = exact(x)
    meas_out[...] = dot(hi, perm[1]) + dot(mid, perm[1]) + dot(low, perm[1])


def whole_patch(off, own, below, right, diag):
    qr, tr = off[0] // W, off[0] % W
    qc, tc = off[1] // W, off[1] % W
    rho, gam = iotas()
    low_r, low_c = rho < tr, gam < tc
    halo_r = rho < tr * qr
    halo_c = gam < tc * qc
    below_v = jnp.where(low_c, below[:, W:], below[:, block(qc)])
    right_v = jnp.where(low_r, right[W:, :], right[block(qr), :])
    out = jnp.where(halo_r, below_v, own)
    return jnp.where(halo_c, jnp.where(halo_r, diag[...], right_v), out)


def put_pair(s, first, second, keep_out, send_out):
    keep_out[...] = jnp.where(s == 0, first, second)
    send_out[...] = jnp.where(s == 0, second, first)


def gradient_kernel(
    scal, own, b0, r0, d0, b1, r1, d1, probe, meas, tab,
    keep_out, send_out, probe_keep_out, probe_send_out,
    obj, back, far, modes,
):
    s, tr, tc = scal[2], scal[0] % W, scal[1] % W
    for layer in range(2):
        for plane, halo in ((s, (b0, r0, d0)), (1 - s, (b1, r1, d1))):
            parts = [h.at[layer] for h in halo]
            obj[layer, plane] = whole_patch(scal, own[layer, plane], *parts)
    for m in range(2):
        re, im = cmul(probe[m, 0], probe[m, 1], obj[0, 0], obj[0, 1])
        back[m, 0], back[m, 1] = both_axes(tab, "prop", re, im)
    for m in range(2):
        re, im = cmul(back[m, 0], back[m, 1], obj[1, 0], obj[1, 1])
        far[m, 0], far[m, 1] = both_axes(tab, "fwd", re, im)
    inten = far[0, 0] ** 2 + far[0, 1] ** 2 + far[1, 0] ** 2 + far[1, 1] ** 2
    resid = 2.0 * (inten - meas[...])
    g_r = g_i = None
    for m in range(2):
        re, im = both_axes(tab, "inv", resid * far[m, 0], resid * far[m, 1])
        a, b = cmul_conj(back[m, 0], back[m, 1], re, im)
        g_r, g_i = (a, b) if g_r is None else (g_r + a, g_i + b)
        modes[m, 0], modes[m, 1] = cmul_conj(obj[1, 0], obj[1, 1], re, im)
    put_pair(s, g_r, g_i, keep_out.at[1], send_out.at[1])
    g_r = g_i = None
    for m in range(2):
        re, im = both_axes(tab, "back", modes[m, 0], modes[m, 1])
        a, b = cmul_conj(probe[m, 0], probe[m, 1], re, im)
        g_r, g_i = (a, b) if g_r is None else (g_r + a, g_i + b)
        for p, x in enumerate(cmul_conj(obj[0, 0], obj[0, 1], re, im)):
            x = pltpu.roll(x * (1.0 / 256.0), (W - tr) % W, 0)
            modes[m, p] = pltpu.roll(x, (W - tc) % W, 1)
    put_pair(s, g_r, g_i, keep_out.at[0], send_out.at[0])
    put_pair(s, modes[0], modes[1], probe_keep_out, probe_send_out)


def spread_kernel(scal, mine, other, own_out, below_out, right0, right1, diag_out):
    rho, gam = iotas()

    def band(index, q, t, i):
        return ((index >= t) & (q == i)) | ((index < t) & (q + 1 == i))

    where = []
    for k in range(2):
        r, c = scal[2 * k], scal[2 * k + 1]
        rows = [band(rho, r // W, r % W, i) for i in range(3)]
        cols = [band(gam, c // W, c % W, j) for j in range(3)]
        where.append((rows, cols))
    for i in range(3):
        for j in range(3):
            here = [r[i] & c[j] for r, c in where]
            for k in range(2):
                v = jnp.where(here[0], mine[k], 0.0) + jnp.where(here[1], other[k], 0.0)
                if i < 2 and j < 2:
                    own_out[k, i * W : (i + 1) * W, j * W : (j + 1) * W] = v
                elif i < 2:
                    (right0, right1)[k][i * W : (i + 1) * W, :] = v
                elif j < 2:
                    below_out[k, :, j * W : (j + 1) * W] = v
                else:
                    diag_out[k] = v


def finish_kernel(scal, own0, b0, r00, r01, d0, own1, b1, r10, r11, d1, out):
    s = scal[0]
    for k in range(2):
        mine = (own0, b0, (r00, r01)[k], d0)
        other = (own1, b1, (r10, r11)[k], d1)
        for plane, (own, b, r, d) in ((s, mine), (1 - s, other)):
            out[k, plane, W:, W:] = own[k, W:, W:]
            out[k, plane, :W, :W] = own[k, :W, :W] + (b[k, :, :W] + r[:W, :] + d[k])
            out[k, plane, :W, W:] = own[k, :W, W:] + b[k, :, W:]
            out[k, plane, W:, :W] = own[k, W:, :W] + r[W:, :]


def place_kernel(scal, *refs):
    parts, out = refs[:-1], refs[-1]
    for d, part in enumerate(parts):
        out[scal[0] ^ d] = part[...]


LIMIT = 8 * 2**20


def call(kernel, outs, args, flops=0, scratch=()):
    spec = pl.BlockSpec(memory_space=pltpu.VMEM)
    moved = 4 * sum(math.prod(o) for o in outs) + sum(a.size * a.dtype.itemsize for a in args)
    return pl.pallas_call(
        kernel,
        out_shape=[jax.ShapeDtypeStruct(o, F32) for o in outs],
        in_specs=[pl.BlockSpec(memory_space=pltpu.SMEM)] + [spec] * (len(args) - 1),
        out_specs=[spec] * len(outs),
        scratch_shapes=[pltpu.VMEM(s, F32) for s in scratch],
        compiler_params=pltpu.CompilerParams(vmem_limit_bytes=LIMIT),
        cost_estimate=pl.CostEstimate(flops=flops, bytes_accessed=moved, transcendentals=0),
    )(*args)


def swap(x):
    return lax.ppermute(x, "scan", [(0, 1), (1, 0)])


def shift(x, rows, cols):
    n_a, n_b = lax.axis_size("tx"), lax.axis_size("ty")
    route = [
        (a * n_b + b, (a + rows) * n_b + b + cols)
        for a in range(n_a)
        for b in range(n_b)
        if 0 <= a + rows < n_a and 0 <= b + cols < n_b
    ]
    return lax.ppermute(x, ("tx", "ty"), route)


def at(v, i):
    return lax.dynamic_index_in_dim(v, i, 0, keepdims=False)


def exchange(x, axis, bits):
    return lax.ppermute(x, axis, [(i, i ^ bits) for i in range(lax.axis_size(axis))])


def scatter_sum(v, index, unit):
    got = [exchange(at(v, index ^ d), "ty", d * unit) for d in (1, 2, 3)]
    return at(v, index) + ((got[0] + got[1]) + got[2])


def gather(v, index, unit):
    got = [v] + [exchange(v, "ty", d * unit) for d in (1, 2, 3)]
    return call(place_kernel, [(4,) + v.shape], (index[None], *got))[0]


def after(x, *others):
    return lax.optimization_barrier((x,) + others)[0]


def body(object_slices, probe_modes, offsets, measured):
    s = lax.axis_index("scan").astype(jnp.int32)
    col = lax.axis_index("ty")
    x, y = col // 4, col % 4
    tab = jnp.asarray(tables())
    perm = jnp.asarray(deinterleave())
    off = offsets.reshape(2)
    off_other = swap(off)
    scal = jnp.concatenate([off, s[None]])
    pair = jnp.concatenate([off, off_other])

    def strip(rows, cols):
        zero = jnp.int32(0)
        cut = lax.dynamic_slice(object_slices, (zero, s, zero, zero), (2, 1, rows, cols))
        return cut.reshape(2, rows, cols)

    mine = [
        shift(strip(W, 2 * W), -1, 0),
        shift(strip(2 * W, W), 0, -1),
        shift(strip(W, W), -1, -1),
    ]
    own, probe, meas = call(
        prep_kernel,
        [(2, 2, W, W), (2, 2, W, W), (W, W)],
        (off, object_slices, probe_modes, measured[0], perm),
        flops=12 * W**3,
    )
    mine = [after(h, own) for h in mine]
    keep, send, probe_keep, probe_send = call(
        gradient_kernel,
        [(2, W, W), (2, W, W), (2, W, W), (2, W, W)],
        (scal, own, *mine, *[swap(h) for h in mine], probe, meas, tab),
        flops=192 * W**3,
        scratch=[(2, 2, W, W)] * 4,
    )
    own_sum, below, right0, right1, diag = call(
        spread_kernel,
        [(2, 2 * W, 2 * W), (2, W, 2 * W), (2 * W, W), (2 * W, W), (2, W, W)],
        (pair, keep, swap(send)),
    )

    v = probe_keep + swap(probe_send)
    below = shift(below, 1, 0)
    right1 = shift(right1, 0, 1)
    v = scatter_sum(v.reshape(4, W // 2, W), x, 4)
    v = after(v, right1)
    v = scatter_sum(v.reshape(4, W // 8, W), y, 1)
    v = after(v, below, right1)
    right0 = shift(after(right0, v), 0, 1)
    for bit in (1, 2, 4):
        v = v + exchange(v, "tx", bit)
    v = after(v, right0)
    v = gather(v, y, 1).reshape(W // 2, W)
    diag = shift(after(diag, v), 1, 1)
    v = gather(v, x, 4).reshape(2, W, W)
    grad_probe = call(place_kernel, [(2, 2, W, W)], (s[None], v, swap(v)))[0]
    mine = (own_sum, below, right0, right1, diag)
    tile = call(
        finish_kernel, [(2, 2, 2 * W, 2 * W)], (s[None], *mine, *[swap(t) for t in mine])
    )[0]
    return tile, grad_probe


def solution(mesh):
    placed = (
        P(None, None, "tx", "ty"),
        P(),
        P(("tx", "ty", "scan"), None),
        P(("tx", "ty", "scan"), None, None),
    )
    return jax.shard_map(
        body,
        mesh=mesh,
        in_specs=placed,
        out_specs=(P(None, None, "tx", "ty"), P()),
        check_vma=False,
    )
```

```python
import functools
import math

import jax
import jax.numpy as jnp
import ml_dtypes
import numpy as np
from jax import lax
from jax.experimental import pallas as pl
from jax.experimental.pallas import tpu as pltpu
from jax.sharding import PartitionSpec as P

fresnel_number = 6.0
W = 256
B16 = jnp.bfloat16
F32 = jnp.float32


def real_form(matrix):
    return np.block([[matrix.real, -matrix.imag], [matrix.imag, matrix.real]])


def tables():
    half = W // 2
    n = np.arange(half)
    norm = 1.0 / math.sqrt(W)
    even = np.exp(-2j * np.pi * np.outer(2 * n, n) / W) * norm
    odd = np.exp(-2j * np.pi * np.outer(2 * n + 1, n) / W) * norm
    k = np.arange(W)
    q = (k + half) % W - half
    h = np.exp(-1j * np.pi * fresnel_number * q.astype(np.float64) ** 2 / float(W * W))
    taps = np.fft.ifft(h)
    diff = (n[:, None] - n[None, :]) % W
    near, far = taps[diff], taps[(diff + half) % W]
    mats = [even, odd, 0.5 * (near + far), 0.5 * (near - far)]
    forms = []
    for m in mats:
        r = real_form(m)
        forms += [r, r.T]
    full = np.stack(forms)
    hi = full.astype(ml_dtypes.bfloat16)
    lo = (full - hi.astype(np.float64)).astype(ml_dtypes.bfloat16)
    return np.stack([hi, lo], axis=1)


E_L, E_T, O_L, O_T, U_L, U_T, V_L, V_T = range(8)


def deinterleave():
    order = np.concatenate([np.arange(0, W, 2), np.arange(1, W, 2)])
    p = np.zeros((W, W), np.float32)
    p[np.arange(W), order] = 1.0
    return np.stack([p, p.T]).astype(ml_dtypes.bfloat16)


def dot(a, b):
    return jnp.dot(a, b, preferred_element_type=F32)


def split(x):
    hi = x.astype(B16)
    return hi, (x - hi.astype(F32)).astype(B16)


def times(tab, which, x, axis):
    hi, lo = split(x)
    t_hi, t_lo = tab[which, 0], tab[which, 1]
    if axis == 0:
        return dot(t_hi, hi) + (dot(t_hi, lo) + dot(t_lo, hi))
    return dot(hi, t_hi) + (dot(lo, t_hi) + dot(hi, t_lo))


def halves(x, axis):
    h = W // 2
    return (x[:h], x[h:]) if axis == 0 else (x[:, :h], x[:, h:])


def butterfly(re, im, axis):
    r0, r1 = halves(re, axis)
    i0, i1 = halves(im, axis)
    u = jnp.concatenate([r0 + r1, i0 + i1], axis)
    v = jnp.concatenate([r0 - r1, i0 - i1], axis)
    return u, v


def join(a, b, axis):
    ar, ai = halves(a, axis)
    br, bi = halves(b, axis)
    return jnp.concatenate([ar, br], axis), jnp.concatenate([ai, bi], axis)


def one_axis(tab, kind, re, im, axis):
    left = axis == 0
    if kind == "inv":
        r0, r1 = halves(re, axis)
        i0, i1 = halves(im, axis)
        u, v = jnp.concatenate([r0, i0], axis), jnp.concatenate([r1, i1], axis)
    else:
        u, v = butterfly(re, im, axis)
    pick = {
        "fwd": (E_L, O_L) if left else (E_T, O_T),
        "inv": (E_T, O_T) if left else (E_L, O_L),
        "prop": (U_L, V_L) if left else (U_T, V_T),
        "back": (U_T, V_T) if left else (U_L, V_L),
    }[kind]
    a = times(tab, pick[0], u, axis)
    b = times(tab, pick[1], v, axis)
    if kind != "fwd":
        a, b = a + b, a - b
    return join(a, b, axis)


def both_axes(tab, kind, re, im):
    re, im = one_axis(tab, kind, re, im, 0)
    return one_axis(tab, kind, re, im, 1)


def cmul(ar, ai, br, bi):
    return ar * br - ai * bi, ar * bi + ai * br


def cmul_conj(ar, ai, br, bi):
    return ar * br + ai * bi, ar * bi - ai * br


def iotas():
    return (
        lax.broadcasted_iota(jnp.int32, (W, W), 0),
        lax.broadcasted_iota(jnp.int32, (W, W), 1),
    )


def block(q):
    return pl.ds(pl.multiple_of(q * W, W), W)


def prep_kernel(off, obj, probe, meas, perm, own_out, probe_out, meas_out):
    qr, tr = off[0] // W, off[0] % W
    qc, tc = off[1] // W, off[1] % W
    rho, gam = iotas()
    low_r, low_c = rho < tr, gam < tc
    for layer in range(2):
        for p in range(2):
            a = jnp.where(low_c, obj[layer, p, block(qr), W:], obj[layer, p, block(qr), block(qc)])
            b = jnp.where(low_c, obj[layer, p, W:, W:], obj[layer, p, W:, block(qc)])
            own_out[layer, p] = jnp.where(low_r, b, a)
    for m in range(2):
        for p in range(2):
            x = pltpu.roll(probe[m, p], tr, 0)
            probe_out[m, p] = pltpu.roll(x, tc, 1)

    def exact(x):
        hi = x.astype(B16)
        rest = x - hi.astype(F32)
        mid = rest.astype(B16)
        return hi, mid, (rest - mid.astype(F32)).astype(B16)

    hi, mid, low = exact(meas[...])
    x = dot(perm[0], hi) + dot(perm[0], mid) + dot(perm[0], low)
    hi, mid, low = exact(x)
    meas_out[...] = dot(hi, perm[1]) + dot(mid, perm[1]) + dot(low, perm[1])


def whole_patch(off, own, below, right, diag):
    qr, tr = off[0] // W, off[0] % W
    qc, tc = off[1] // W, off[1] % W
    rho, gam = iotas()
    low_r, low_c = rho < tr, gam < tc
    halo_r = rho < tr * qr
    halo_c = gam < tc * qc
    below_v = jnp.where(low_c, below[:, W:], below[:, block(qc)])
    right_v = jnp.where(low_r, right[W:, :], right[block(qr), :])
    out = jnp.where(halo_r, below_v, own)
    return jnp.where(halo_c, jnp.where(halo_r, diag[...], right_v), out)


def put_pair(s, first, second, keep_out, send_out):
    keep_out[...] = jnp.where(s == 0, first, second)
    send_out[...] = jnp.where(s == 0, second, first)


def gradient_kernel(
    scal, own, b0, r0, d0, b1, r1, d1, probe, meas, tab,
    keep_out, send_out, probe_keep_out, probe_send_out,
    obj, back, far, modes,
):
    s, tr, tc = scal[2], scal[0] % W, scal[1] % W
    for layer in range(2):
        for plane, halo in ((s, (b0, r0, d0)), (1 - s, (b1, r1, d1))):
            parts = [h.at[layer] for h in halo]
            obj[layer, plane] = whole_patch(scal, own[layer, plane], *parts)
    for m in range(2):
        re, im = cmul(probe[m, 0], probe[m, 1], obj[0, 0], obj[0, 1])
        back[m, 0], back[m, 1] = both_axes(tab, "prop", re, im)
    for m in range(2):
        re, im = cmul(back[m, 0], back[m, 1], obj[1, 0], obj[1, 1])
        far[m, 0], far[m, 1] = both_axes(tab, "fwd", re, im)
    inten = far[0, 0] ** 2 + far[0, 1] ** 2 + far[1, 0] ** 2 + far[1, 1] ** 2
    resid = 2.0 * (inten - meas[...])
    g_r = g_i = None
    for m in range(2):
        re, im = both_axes(tab, "inv", resid * far[m, 0], resid * far[m, 1])
        a, b = cmul_conj(back[m, 0], back[m, 1], re, im)
        g_r, g_i = (a, b) if g_r is None else (g_r + a, g_i + b)
        modes[m, 0], modes[m, 1] = cmul_conj(obj[1, 0], obj[1, 1], re, im)
    put_pair(s, g_r, g_i, keep_out.at[1], send_out.at[1])
    g_r = g_i = None
    for m in range(2):
        re, im = both_axes(tab, "back", modes[m, 0], modes[m, 1])
        a, b = cmul_conj(probe[m, 0], probe[m, 1], re, im)
        g_r, g_i = (a, b) if g_r is None else (g_r + a, g_i + b)
        for p, x in enumerate(cmul_conj(obj[0, 0], obj[0, 1], re, im)):
            x = pltpu.roll(x * (1.0 / 256.0), (W - tr) % W, 0)
            modes[m, p] = pltpu.roll(x, (W - tc) % W, 1)
    put_pair(s, g_r, g_i, keep_out.at[0], send_out.at[0])
    put_pair(s, modes[0], modes[1], probe_keep_out, probe_send_out)


def spread_kernel(scal, mine, other, own_out, below_out, right0, right1, diag_out):
    rho, gam = iotas()

    def band(index, q, t, i):
        return ((index >= t) & (q == i)) | ((index < t) & (q + 1 == i))

    where = []
    for k in range(2):
        r, c = scal[2 * k], scal[2 * k + 1]
        rows = [band(rho, r // W, r % W, i) for i in range(3)]
        cols = [band(gam, c // W, c % W, j) for j in range(3)]
        where.append((rows, cols))
    for i in range(3):
        for j in range(3):
            here = [r[i] & c[j] for r, c in where]
            for k in range(2):
                v = jnp.where(here[0], mine[k], 0.0) + jnp.where(here[1], other[k], 0.0)
                if i < 2 and j < 2:
                    own_out[k, i * W : (i + 1) * W, j * W : (j + 1) * W] = v
                elif i < 2:
                    (right0, right1)[k][i * W : (i + 1) * W, :] = v
                elif j < 2:
                    below_out[k, :, j * W : (j + 1) * W] = v
                else:
                    diag_out[k] = v


def finish_kernel(scal, own0, b0, r00, r01, own1, b1, r10, r11, out, part):
    s = scal[0]
    for k in range(2):
        mine = (own0, b0, (r00, r01)[k])
        other = (own1, b1, (r10, r11)[k])
        for plane, (own, b, r) in ((s, mine), (1 - s, other)):
            out[k, plane, W:, W:] = own[k, W:, W:]
            part[k, plane] = own[k, :W, :W] + (b[k, :, :W] + r[:W, :])
            out[k, plane, :W, W:] = own[k, :W, W:] + b[k, :, W:]
            out[k, plane, W:, :W] = own[k, W:, :W] + r[W:, :]


def corner_kernel(scal, mine, other, part, tile, out):
    s = scal[0]
    for k in range(2):
        out[k, s] = part[k, s] + mine[k]
        out[k, 1 - s] = part[k, 1 - s] + other[k]


def add_corner(s, mine, other, part, tile):
    spec = pl.BlockSpec(memory_space=pltpu.VMEM)
    return pl.pallas_call(
        corner_kernel,
        grid=(1,),
        out_shape=jax.ShapeDtypeStruct(tile.shape, F32),
        in_specs=[pl.BlockSpec(memory_space=pltpu.SMEM), spec, spec, spec]
        + [pl.BlockSpec(memory_space=pl.ANY)],
        out_specs=pl.BlockSpec((2, 2, W, W), lambda i: (0, 0, 0, 0)),
        input_output_aliases={4: 0},
        compiler_params=pltpu.CompilerParams(vmem_limit_bytes=LIMIT),
        cost_estimate=pl.CostEstimate(flops=0, bytes_accessed=2**21, transcendentals=0),
    )(s[None], mine, other, part, tile)


def place_kernel(scal, *refs):
    parts, out = refs[:-1], refs[-1]
    for d, part in enumerate(parts):
        out[scal[0] ^ d] = part[...]


LIMIT = 8 * 2**20


def call(kernel, outs, args, flops=0, scratch=()):
    spec = pl.BlockSpec(memory_space=pltpu.VMEM)
    moved = 4 * sum(math.prod(o) for o in outs) + sum(a.size * a.dtype.itemsize for a in args)
    return pl.pallas_call(
        kernel,
        out_shape=[jax.ShapeDtypeStruct(o, F32) for o in outs],
        in_specs=[pl.BlockSpec(memory_space=pltpu.SMEM)] + [spec] * (len(args) - 1),
        out_specs=[spec] * len(outs),
        scratch_shapes=[pltpu.VMEM(s, F32) for s in scratch],
        compiler_params=pltpu.CompilerParams(vmem_limit_bytes=LIMIT),
        cost_estimate=pl.CostEstimate(flops=flops, bytes_accessed=moved, transcendentals=0),
    )(*args)


def swap(x):
    return lax.ppermute(x, "scan", [(0, 1), (1, 0)])


def shift(x, rows, cols):
    n_a, n_b = lax.axis_size("tx"), lax.axis_size("ty")
    route = [
        (a * n_b + b, (a + rows) * n_b + b + cols)
        for a in range(n_a)
        for b in range(n_b)
        if 0 <= a + rows < n_a and 0 <= b + cols < n_b
    ]
    return lax.ppermute(x, ("tx", "ty"), route)


def at(v, i):
    return lax.dynamic_index_in_dim(v, i, 0, keepdims=False)


def exchange(x, axis, bits):
    return lax.ppermute(x, axis, [(i, i ^ bits) for i in range(lax.axis_size(axis))])


def scatter_sum(v, index, unit):
    got = [exchange(at(v, index ^ d), "ty", d * unit) for d in (1, 2, 3)]
    return at(v, index) + ((got[0] + got[1]) + got[2])


def gather(v, index, unit):
    got = [v] + [exchange(v, "ty", d * unit) for d in (1, 2, 3)]
    return call(place_kernel, [(4,) + v.shape], (index[None], *got))[0]


def after(x, *others):
    return lax.optimization_barrier((x,) + others)[0]


def body(object_slices, probe_modes, offsets, measured):
    s = lax.axis_index("scan").astype(jnp.int32)
    col = lax.axis_index("ty")
    x, y = col // 4, col % 4
    tab = jnp.asarray(tables())
    perm = jnp.asarray(deinterleave())
    off = offsets.reshape(2)
    off_other = swap(off)
    scal = jnp.concatenate([off, s[None]])
    pair = jnp.concatenate([off, off_other])

    def strip(rows, cols):
        zero = jnp.int32(0)
        cut = lax.dynamic_slice(object_slices, (zero, s, zero, zero), (2, 1, rows, cols))
        return cut.reshape(2, rows, cols)

    mine = [
        shift(strip(W, 2 * W), -1, 0),
        shift(strip(2 * W, W), 0, -1),
        shift(strip(W, W), -1, -1),
    ]
    own, probe, meas = call(
        prep_kernel,
        [(2, 2, W, W), (2, 2, W, W), (W, W)],
        (off, object_slices, probe_modes, measured[0], perm),
        flops=12 * W**3,
    )
    mine = [after(h, own) for h in mine]
    keep, send, probe_keep, probe_send = call(
        gradient_kernel,
        [(2, W, W), (2, W, W), (2, W, W), (2, W, W)],
        (scal, own, *mine, *[swap(h) for h in mine], probe, meas, tab),
        flops=192 * W**3,
        scratch=[(2, 2, W, W)] * 4,
    )
    own_sum, below, right0, right1, diag = call(
        spread_kernel,
        [(2, 2 * W, 2 * W), (2, W, 2 * W), (2 * W, W), (2 * W, W), (2, W, W)],
        (pair, keep, swap(send)),
    )

    v = probe_keep + swap(probe_send)
    below = shift(below, 1, 0)
    right1 = shift(right1, 0, 1)
    v = scatter_sum(v.reshape(4, W // 2, W), x, 4)
    v = after(v, right1)
    v = scatter_sum(v.reshape(4, W // 8, W), y, 1)
    v = after(v, below, right1)
    others = [swap(t) for t in (own_sum, below, right1)]
    right0 = shift(after(right0, v), 0, 1)
    for bit in (1, 2, 4):
        v = v + exchange(v, "tx", bit)
    v = after(v, right0, *others)
    v = gather(v, y, 1).reshape(W // 2, W)
    diag = shift(after(diag, v), 1, 1)
    own_o, below_o, right1_o = others
    tile, part = call(
        finish_kernel,
        [(2, 2, 2 * W, 2 * W), (2, 2, W, W)],
        (s[None], own_sum, below, right0, right1, own_o, below_o, swap(right0), right1_o),
    )
    v = after(gather(v, x, 4), part).reshape(2, W, W)
    grad_probe = call(place_kernel, [(2, 2, W, W)], (s[None], v, swap(v)))[0]
    return add_corner(s, diag, swap(diag), part, tile), grad_probe


def solution(mesh):
    placed = (
        P(None, None, "tx", "ty"),
        P(),
        P(("tx", "ty", "scan"), None),
        P(("tx", "ty", "scan"), None, None),
    )
    return jax.shard_map(
        body,
        mesh=mesh,
        in_specs=placed,
        out_specs=(P(None, None, "tx", "ty"), P()),
        check_vma=False,
    )
```

```python
import functools
import math

import jax
import jax.numpy as jnp
import ml_dtypes
import numpy as np
from jax import lax
from jax.experimental import pallas as pl
from jax.experimental.pallas import tpu as pltpu
from jax.sharding import PartitionSpec as P

fresnel_number = 6.0
W = 256
B16 = jnp.bfloat16
F32 = jnp.float32


def real_form(matrix):
    return np.block([[matrix.real, -matrix.imag], [matrix.imag, matrix.real]])


def tables():
    half = W // 2
    n = np.arange(half)
    norm = 1.0 / math.sqrt(W)
    even = np.exp(-2j * np.pi * np.outer(2 * n, n) / W) * norm
    odd = np.exp(-2j * np.pi * np.outer(2 * n + 1, n) / W) * norm
    k = np.arange(W)
    q = (k + half) % W - half
    h = np.exp(-1j * np.pi * fresnel_number * q.astype(np.float64) ** 2 / float(W * W))
    taps = np.fft.ifft(h)
    diff = (n[:, None] - n[None, :]) % W
    near, far = taps[diff], taps[(diff + half) % W]
    mats = [even, odd, 0.5 * (near + far), 0.5 * (near - far)]
    forms = []
    for m in mats:
        r = real_form(m)
        forms += [r, r.T]
    full = np.stack(forms)
    hi = full.astype(ml_dtypes.bfloat16)
    lo = (full - hi.astype(np.float64)).astype(ml_dtypes.bfloat16)
    return np.stack([hi, lo], axis=1)


E_L, E_T, O_L, O_T, U_L, U_T, V_L, V_T = range(8)


def deinterleave():
    order = np.concatenate([np.arange(0, W, 2), np.arange(1, W, 2)])
    p = np.zeros((W, W), np.float32)
    p[np.arange(W), order] = 1.0
    return np.stack([p, p.T]).astype(ml_dtypes.bfloat16)


def dot(a, b):
    return jnp.dot(a, b, preferred_element_type=F32)


def split(x):
    hi = x.astype(B16)
    return hi, (x - hi.astype(F32)).astype(B16)


def times(tab, which, x, axis):
    hi, lo = split(x)
    t_hi, t_lo = tab[which, 0], tab[which, 1]
    if axis == 0:
        return dot(t_hi, hi) + (dot(t_hi, lo) + dot(t_lo, hi))
    return dot(hi, t_hi) + (dot(lo, t_hi) + dot(hi, t_lo))


def halves(x, axis):
    h = W // 2
    return (x[:h], x[h:]) if axis == 0 else (x[:, :h], x[:, h:])


def butterfly(re, im, axis):
    r0, r1 = halves(re, axis)
    i0, i1 = halves(im, axis)
    u = jnp.concatenate([r0 + r1, i0 + i1], axis)
    v = jnp.concatenate([r0 - r1, i0 - i1], axis)
    return u, v


def join(a, b, axis):
    ar, ai = halves(a, axis)
    br, bi = halves(b, axis)
    return jnp.concatenate([ar, br], axis), jnp.concatenate([ai, bi], axis)


def one_axis(tab, kind, re, im, axis):
    left = axis == 0
    if kind == "inv":
        r0, r1 = halves(re, axis)
        i0, i1 = halves(im, axis)
        u, v = jnp.concatenate([r0, i0], axis), jnp.concatenate([r1, i1], axis)
    else:
        u, v = butterfly(re, im, axis)
    pick = {
        "fwd": (E_L, O_L) if left else (E_T, O_T),
        "inv": (E_T, O_T) if left else (E_L, O_L),
        "prop": (U_L, V_L) if left else (U_T, V_T),
        "back": (U_T, V_T) if left else (U_L, V_L),
    }[kind]
    a = times(tab, pick[0], u, axis)
    b = times(tab, pick[1], v, axis)
    if kind != "fwd":
        a, b = a + b, a - b
    return join(a, b, axis)


def both_axes(tab, kind, re, im):
    re, im = one_axis(tab, kind, re, im, 0)
    return one_axis(tab, kind, re, im, 1)


def cmul(ar, ai, br, bi):
    return ar * br - ai * bi, ar * bi + ai * br


def cmul_conj(ar, ai, br, bi):
    return ar * br + ai * bi, ar * bi - ai * br


def iotas():
    return (
        lax.broadcasted_iota(jnp.int32, (W, W), 0),
        lax.broadcasted_iota(jnp.int32, (W, W), 1),
    )


def block(q):
    return pl.ds(pl.multiple_of(q * W, W), W)


def prep_kernel(off, obj, probe, meas, perm, own_out, probe_out, meas_out):
    qr, tr = off[0] // W, off[0] % W
    qc, tc = off[1] // W, off[1] % W
    rho, gam = iotas()
    low_r, low_c = rho < tr, gam < tc
    for layer in range(2):
        for p in range(2):
            a = jnp.where(low_c, obj[layer, p, block(qr), W:], obj[layer, p, block(qr), block(qc)])
            b = jnp.where(low_c, obj[layer, p, W:, W:], obj[layer, p, W:, block(qc)])
            own_out[layer, p] = jnp.where(low_r, b, a)
    for m in range(2):
        for p in range(2):
            x = pltpu.roll(probe[m, p], tr, 0)
            probe_out[m, p] = pltpu.roll(x, tc, 1)

    def exact(x):
        hi = x.astype(B16)
        rest = x - hi.astype(F32)
        mid = rest.astype(B16)
        return hi, mid, (rest - mid.astype(F32)).astype(B16)

    hi, mid, low = exact(meas[...])
    x = dot(perm[0], hi) + dot(perm[0], mid) + dot(perm[0], low)
    hi, mid, low = exact(x)
    meas_out[...] = dot(hi, perm[1]) + dot(mid, perm[1]) + dot(low, perm[1])


def whole_patch(off, own, below, right, diag):
    qr, tr = off[0] // W, off[0] % W
    qc, tc = off[1] // W, off[1] % W
    rho, gam = iotas()
    low_r, low_c = rho < tr, gam < tc
    halo_r = rho < tr * qr
    halo_c = gam < tc * qc
    below_v = jnp.where(low_c, below[:, W:], below[:, block(qc)])
    right_v = jnp.where(low_r, right[W:, :], right[block(qr), :])
    out = jnp.where(halo_r, below_v, own)
    return jnp.where(halo_c, jnp.where(halo_r, diag[...], right_v), out)


def put_pair(s, first, second, keep_out, send_out):
    keep_out[...] = jnp.where(s == 0, first, second)
    send_out[...] = jnp.where(s == 0, second, first)


def gradient_kernel(
    scal, own, b0, r0, d0, b1, r1, d1, probe, meas, tab,
    keep_out, send_out, probe_keep_out, probe_send_out,
    obj, back, far, modes,
):
    s, tr, tc = scal[2], scal[0] % W, scal[1] % W
    for layer in range(2):
        for plane, halo in ((s, (b0, r0, d0)), (1 - s, (b1, r1, d1))):
            parts = [h.at[layer] for h in halo]
            obj[layer, plane] = whole_patch(scal, own[layer, plane], *parts)
    for m in range(2):
        re, im = cmul(probe[m, 0], probe[m, 1], obj[0, 0], obj[0, 1])
        back[m, 0], back[m, 1] = both_axes(tab, "prop", re, im)
    for m in range(2):
        re, im = cmul(back[m, 0], back[m, 1], obj[1, 0], obj[1, 1])
        far[m, 0], far[m, 1] = both_axes(tab, "fwd", re, im)
    inten = far[0, 0] ** 2 + far[0, 1] ** 2 + far[1, 0] ** 2 + far[1, 1] ** 2
    resid = 2.0 * (inten - meas[...])
    g_r = g_i = None
    for m in range(2):
        re, im = both_axes(tab, "inv", resid * far[m, 0], resid * far[m, 1])
        a, b = cmul_conj(back[m, 0], back[m, 1], re, im)
        g_r, g_i = (a, b) if g_r is None else (g_r + a, g_i + b)
        modes[m, 0], modes[m, 1] = cmul_conj(obj[1, 0], obj[1, 1], re, im)
    put_pair(s, g_r, g_i, keep_out.at[1], send_out.at[1])
    g_r = g_i = None
    for m in range(2):
        re, im = both_axes(tab, "back", modes[m, 0], modes[m, 1])
        a, b = cmul_conj(probe[m, 0], probe[m, 1], re, im)
        g_r, g_i = (a, b) if g_r is None else (g_r + a, g_i + b)
        for p, x in enumerate(cmul_conj(obj[0, 0], obj[0, 1], re, im)):
            x = pltpu.roll(x * (1.0 / 256.0), (W - tr) % W, 0)
            modes[m, p] = pltpu.roll(x, (W - tc) % W, 1)
    put_pair(s, g_r, g_i, keep_out.at[0], send_out.at[0])
    put_pair(s, modes[0], modes[1], probe_keep_out, probe_send_out)


def spread_kernel(scal, mine, other, own_out, below_out, right0, right1, diag_out):
    rho, gam = iotas()

    def band(index, q, t, i):
        return ((index >= t) & (q == i)) | ((index < t) & (q + 1 == i))

    where = []
    for k in range(2):
        r, c = scal[2 * k], scal[2 * k + 1]
        rows = [band(rho, r // W, r % W, i) for i in range(3)]
        cols = [band(gam, c // W, c % W, j) for j in range(3)]
        where.append((rows, cols))
    for i in range(3):
        for j in range(3):
            here = [r[i] & c[j] for r, c in where]
            for k in range(2):
                v = jnp.where(here[0], mine[k], 0.0) + jnp.where(here[1], other[k], 0.0)
                if i < 2 and j < 2:
                    own_out[k, i * W : (i + 1) * W, j * W : (j + 1) * W] = v
                elif i < 2:
                    (right0, right1)[k][i * W : (i + 1) * W, :] = v
                elif j < 2:
                    below_out[k, :, j * W : (j + 1) * W] = v
                else:
                    diag_out[k] = v


def finish_kernel(scal, own0, b0, r00, r01, own1, b1, r10, r11, out, part):
    s = scal[0]
    for k in range(2):
        mine = (own0, b0, (r00, r01)[k])
        other = (own1, b1, (r10, r11)[k])
        for plane, (own, b, r) in ((s, mine), (1 - s, other)):
            out[k, plane, W:, W:] = own[k, W:, W:]
            part[k, plane] = own[k, :W, :W] + (b[k, :, :W] + r[:W, :])
            out[k, plane, :W, W:] = own[k, :W, W:] + b[k, :, W:]
            out[k, plane, W:, :W] = own[k, W:, :W] + r[W:, :]


def corner_kernel(scal, mine, other, part, tile, out):
    s = scal[0]
    for k in range(2):
        out[k, s] = part[k, s] + mine[k]
        out[k, 1 - s] = part[k, 1 - s] + other[k]


def add_corner(s, mine, other, part, tile):
    spec = pl.BlockSpec(memory_space=pltpu.VMEM)
    return pl.pallas_call(
        corner_kernel,
        grid=(1,),
        out_shape=jax.ShapeDtypeStruct(tile.shape, F32),
        in_specs=[pl.BlockSpec(memory_space=pltpu.SMEM), spec, spec, spec]
        + [pl.BlockSpec(memory_space=pl.ANY)],
        out_specs=pl.BlockSpec((2, 2, W, W), lambda i: (0, 0, 0, 0)),
        input_output_aliases={4: 0},
        compiler_params=pltpu.CompilerParams(vmem_limit_bytes=LIMIT),
        cost_estimate=pl.CostEstimate(flops=0, bytes_accessed=2**21, transcendentals=0),
    )(s[None], mine, other, part, tile)


def place_kernel(scal, *refs):
    parts, out = refs[:-1], refs[-1]
    for d, part in enumerate(parts):
        out[scal[0] ^ d] = part[...]


LIMIT = 8 * 2**20


def call(kernel, outs, args, flops=0, scratch=()):
    spec = pl.BlockSpec(memory_space=pltpu.VMEM)
    moved = 4 * sum(math.prod(o) for o in outs) + sum(a.size * a.dtype.itemsize for a in args)
    return pl.pallas_call(
        kernel,
        out_shape=[jax.ShapeDtypeStruct(o, F32) for o in outs],
        in_specs=[pl.BlockSpec(memory_space=pltpu.SMEM)] + [spec] * (len(args) - 1),
        out_specs=[spec] * len(outs),
        scratch_shapes=[pltpu.VMEM(s, F32) for s in scratch],
        compiler_params=pltpu.CompilerParams(vmem_limit_bytes=LIMIT),
        cost_estimate=pl.CostEstimate(flops=flops, bytes_accessed=moved, transcendentals=0),
    )(*args)


def swap(x):
    return lax.ppermute(x, "scan", [(0, 1), (1, 0)])


def shift(x, rows, cols):
    n_a, n_b = lax.axis_size("tx"), lax.axis_size("ty")
    route = [
        (a * n_b + b, (a + rows) * n_b + b + cols)
        for a in range(n_a)
        for b in range(n_b)
        if 0 <= a + rows < n_a and 0 <= b + cols < n_b
    ]
    return lax.ppermute(x, ("tx", "ty"), route)


def at(v, i):
    return lax.dynamic_index_in_dim(v, i, 0, keepdims=False)


def exchange(x, axis, bits):
    return lax.ppermute(x, axis, [(i, i ^ bits) for i in range(lax.axis_size(axis))])


def scatter_sum(v, index, unit):
    got = [exchange(at(v, index ^ d), "ty", d * unit) for d in (1, 2, 3)]
    return at(v, index) + ((got[0] + got[1]) + got[2])


def gather(v, index, unit):
    got = [v] + [exchange(v, "ty", d * unit) for d in (1, 2, 3)]
    return call(place_kernel, [(4,) + v.shape], (index[None], *got))[0]


def after(x, *others):
    return lax.optimization_barrier((x,) + others)[0]


def body(object_slices, probe_modes, offsets, measured):
    s = lax.axis_index("scan").astype(jnp.int32)
    col = lax.axis_index("ty")
    x, y = col // 4, col % 4
    tab = jnp.asarray(tables())
    perm = jnp.asarray(deinterleave())
    off = offsets.reshape(2)
    off_other = swap(off)
    scal = jnp.concatenate([off, s[None]])
    pair = jnp.concatenate([off, off_other])

    def strip(rows, cols):
        zero = jnp.int32(0)
        cut = lax.dynamic_slice(object_slices, (zero, s, zero, zero), (2, 1, rows, cols))
        return cut.reshape(2, rows, cols)

    mine = [
        shift(strip(W, 2 * W), -1, 0),
        shift(strip(2 * W, W), 0, -1),
        shift(strip(W, W), -1, -1),
    ]
    own, probe, meas = call(
        prep_kernel,
        [(2, 2, W, W), (2, 2, W, W), (W, W)],
        (off, object_slices, probe_modes, measured[0], perm),
        flops=12 * W**3,
    )
    mine = [after(h, own) for h in mine]
    keep, send, probe_keep, probe_send = call(
        gradient_kernel,
        [(2, W, W), (2, W, W), (2, W, W), (2, W, W)],
        (scal, own, *mine, *[swap(h) for h in mine], probe, meas, tab),
        flops=192 * W**3,
        scratch=[(2, 2, W, W)] * 4,
    )
    own_sum, below, right0, right1, diag = call(
        spread_kernel,
        [(2, 2 * W, 2 * W), (2, W, 2 * W), (2 * W, W), (2 * W, W), (2, W, W)],
        (pair, keep, swap(send)),
    )

    v = probe_keep + swap(probe_send)
    below = shift(below, 1, 0)
    right1 = shift(right1, 0, 1)
    v = scatter_sum(v.reshape(4, W // 2, W), x, 4)
    v = after(v, right1)
    v = scatter_sum(v.reshape(4, W // 8, W), y, 1)
    v, own_sum, below, right1 = lax.optimization_barrier((v, own_sum, below, right1))
    others = [swap(t) for t in (own_sum, below, right1)]
    right0 = shift(after(right0, v), 0, 1)
    for bit in (1, 2, 4):
        v = v + exchange(v, "tx", bit)
    v = after(v, right0, *others)
    v = gather(v, y, 1).reshape(W // 2, W)
    diag = shift(after(diag, v), 1, 1)
    own_o, below_o, right1_o = others
    tile, part = call(
        finish_kernel,
        [(2, 2, 2 * W, 2 * W), (2, 2, W, W)],
        (s[None], own_sum, below, right0, right1, own_o, below_o, swap(right0), right1_o),
    )
    v = after(gather(v, x, 4), part).reshape(2, W, W)
    grad_probe = call(place_kernel, [(2, 2, W, W)], (s[None], v, swap(v)))[0]
    return add_corner(s, diag, swap(diag), part, tile), grad_probe


def solution(mesh):
    placed = (
        P(None, None, "tx", "ty"),
        P(),
        P(("tx", "ty", "scan"), None),
        P(("tx", "ty", "scan"), None, None),
    )
    return jax.shard_map(
        body,
        mesh=mesh,
        in_specs=placed,
        out_specs=(P(None, None, "tx", "ty"), P()),
        check_vma=False,
    )
```
